256 devices in a mesh: lat: 32 (over z, y_hi, core), ma: 8 (over x, y_lo).
Axes of the slice: x: 4, y: 4 (y_hi: 2, y_lo: 2; y = y_hi * 2 + y_lo), z: 8, core: 2. Of those that a mesh axis runs over, the one named last changes fastest.
Arguments:
- spectral: bfloat16 [64, 2, 648, 768], P('ma'), may hold values from -0.25 to 0.25
- set_pair: int32 [64], P('ma'), may hold values from 0 to 639, as said below
- lat_sines: float32 [1280], replicated, may hold values from 0.005 to 0.3
Outputs:
- grid: bfloat16 [2560, 64, 2, 768], P(('lat', 'ma'))
The draws below stay inside these ranges and needn't reach their ends.
Inputs may be any that keep to these rules, and one draw needn't show every extreme that they name: `set_pair`: the values are distinct; 0 and 639 both occur.
All inputs are finite; a program needn't handle non-finite values.
Results may differ from the reference program's by a relative error of at most 0.0058.
Values may be sent and summed in bfloat16 or wider, within the bound.
A program may use at most 128 MiB of HBM per device.

```python
import jax
import jax.numpy as jnp
from jax import lax

M = 1280
NH = 648
COLS = 768
MSETS = 64
LATP = 1280


def draw_set_pair(key, part):
    interior = jax.random.permutation(key, M // 2 - 2)[:MSETS - 2] + 1
    chosen = jnp.concatenate([jnp.array([0, M // 2 - 1], dtype=jnp.int32), interior.astype(jnp.int32)])
    placing = jax.random.permutation(jax.random.fold_in(key, 7), MSETS)
    return chosen[placing].astype(jnp.int32)


def steps_of(rng, extent, cuts, low, largest):
    factor_of, own = 1.0, jax.random.fold_in(rng, 6)
    for axis_at, shards_of in cuts:
        heights = jnp.exp(jax.random.uniform(jax.random.fold_in(own, axis_at), (shards_of,), jnp.float32, low / len(cuts), largest / len(cuts)))
        factor_of = factor_of * jnp.repeat(heights, extent[axis_at] // shards_of).reshape([-1 if axis == axis_at else 1 for axis in range(len(extent))])
    return factor_of


def normal_values(own_key, extent, scale, most, split=(), kind=jnp.bfloat16):
    drawn = scale * jax.random.normal(own_key, extent, jnp.float32)
    if split:
        drawn = drawn * steps_of(own_key, extent, split, -0.22, 0.18)
    return jnp.clip(drawn, -most, most).astype(kind)


def setup_inputs(seed: int = 0) -> dict:
    splits = jax.random.split(jax.random.key(seed), 4)
    spectral = normal_values(splits[0], (MSETS, 2, NH, COLS), NH ** -0.5, 0.25, ((0, 8),))
    set_pair = draw_set_pair(jax.random.fold_in(splits[3], 71), 0)
    lat_sines = jnp.clip(jax.random.uniform(splits[2], (LATP,), jnp.float32, 0.005, 0.3), 0.005, 0.3)
    return {"spectral": spectral, "set_pair": set_pair, "lat_sines": lat_sines}


def compose(earlier, later):
    return (later[0] * earlier[0] + later[1] * earlier[2], later[0] * earlier[1] + later[1] * earlier[3], later[2] * earlier[0] + later[3] * earlier[2], later[2] * earlier[1] + later[3] * earlier[3], later[0] * earlier[4] + later[1] * earlier[5] + later[4], later[2] * earlier[4] + later[3] * earlier[5] + later[5])

def legendre_runs(sines, pairs):
    positions = jnp.arange(M + 1, dtype=jnp.int32)[None, :]
    run_length = (M - pairs)[:, None]
    first_run = positions < run_length
    order_m = jnp.where(first_run, pairs[:, None], M - 1 - pairs[:, None]).astype(jnp.float32)
    offset_k = jnp.where(first_run, positions, positions - run_length).astype(jnp.float32)
    degree = order_m + offset_k
    recurring = offset_k > 0.5
    beyond_one = offset_k > 1.5
    prior_degree = degree - 1.0
    factor_a = jnp.sqrt(jnp.where(recurring, 4.0 * degree * degree - 1.0, 1.0) / jnp.where(recurring, degree * degree - order_m * order_m, 1.0))
    factor_b = jnp.sqrt(jnp.where(beyond_one, prior_degree * prior_degree - order_m * order_m, 0.0) / jnp.where(beyond_one, 4.0 * prior_degree * prior_degree - 1.0, 1.0))
    log_start = 0.5 * (lax.lgamma(order_m + 1.5) - lax.lgamma(order_m + 1.0) - lax.lgamma(jnp.ones_like(order_m) * 1.5)) + 0.5 * jnp.log(jnp.ones_like(order_m) * 0.5)
    log_cosine = jnp.log(1.0 - sines * sines)
    full_shape = (pairs.shape[0], sines.shape[0], M + 1)
    start_values = jnp.exp(log_start[:, None, :] + 0.5 * order_m[:, None, :] * log_cosine[None, :, None])
    recur_mask = recurring[:, None, :]
    upper_left = jnp.where(recur_mask, factor_a[:, None, :] * sines[None, :, None], 0.0).astype(jnp.float32)
    upper_right = jnp.broadcast_to(jnp.where(recur_mask, -(factor_a * factor_b)[:, None, :], 0.0), full_shape).astype(jnp.float32)
    lower_left = jnp.broadcast_to(jnp.where(recur_mask, 1.0, 0.0), full_shape).astype(jnp.float32)
    lower_right = jnp.zeros(full_shape, jnp.float32)
    offset_one = jnp.where(recur_mask, 0.0, start_values).astype(jnp.float32)
    offset_two = jnp.zeros(full_shape, jnp.float32)
    scanned = lax.associative_scan(compose, (upper_left, upper_right, lower_left, lower_right, offset_one, offset_two), axis=2)
    return scanned[4]

def parity_weights(values, pairs, parity):
    slot_index = jnp.arange(NH, dtype=jnp.int32)[None, :]
    run_length = (M - pairs)[:, None]
    first_count = (run_length + 1 - parity) // 2
    second_count = (pairs[:, None] + 2 - parity) // 2
    source = jnp.where(slot_index < first_count, 2 * slot_index + parity, run_length + 2 * (slot_index - first_count) + parity)
    source = jnp.clip(source, 0, M).astype(jnp.int32)
    picked = jnp.take_along_axis(values, source[:, None, :], axis=2)
    in_first = (slot_index < first_count)[:, None, :]
    in_second = ((slot_index >= first_count) & (slot_index < first_count + second_count))[:, None, :]
    return jnp.stack([jnp.where(in_first, picked, 0.0), jnp.where(in_second, picked, 0.0)], axis=2).astype(jnp.bfloat16)

def reference(spectral, set_pair, lat_sines):

    def one_set(operands):
        coeffs, pair_index = operands
        values = legendre_runs(lat_sines, pair_index[None])
        partials = []
        for parity in range(2):
            weights = lax.optimization_barrier(parity_weights(values, pair_index[None], parity)[0])
            summed = jnp.einsum('tje,ec->tjc', weights.astype(jnp.float32), coeffs[parity].astype(jnp.float32))
            partials.append(summed.astype(jnp.bfloat16))
        even_part, odd_part = lax.optimization_barrier((partials[0], partials[1]))
        even_sum = even_part.astype(jnp.float32)
        odd_sum = odd_part.astype(jnp.float32)
        return jnp.stack([(even_sum + odd_sum).astype(jnp.bfloat16), (even_sum - odd_sum).astype(jnp.bfloat16)])
    stacked = lax.map(one_set, (spectral, set_pair))
    return stacked.transpose(1, 2, 0, 3, 4).reshape(2 * LATP, MSETS, 2, COLS)
```

```python
import functools
import math

import jax
import jax.numpy as jnp
from jax import lax
from jax.experimental import pallas as pl
from jax.experimental.pallas import tpu as pltpu
from jax.sharding import PartitionSpec as P

M = 1280
NH = 648
COLS = 768
BAND = 80
ROWS = 10
SEG = 81
SETS = 4
MESH = pl.DeviceIdType.MESH
F32, BF16 = jnp.float32, jnp.bfloat16


def step_factors(pair):
    seg = lax.broadcasted_iota(jnp.int32, (8, 128), 0)
    lane = lax.broadcasted_iota(jnp.int32, (8, 128), 1)
    v = seg * SEG + lane
    split = (M + 1 - pair) // 2
    first = v < split
    order = jnp.where(first, pair, M - 1 - pair)
    offset = 2 * jnp.where(first, v, v - split)
    out = []
    for parity in range(2):
        k = (offset + parity).astype(F32)
        m = order.astype(F32)
        n = m + k
        num = 4.0 * n * n - 1.0
        den = k * (n + m)
        recurring = k > 0.5
        a = jnp.sqrt(jnp.where(recurring, num, 0.0) / jnp.where(recurring, den, 1.0))
        beyond = k > 1.5
        q = n - 1.0
        b = jnp.sqrt(
            jnp.where(beyond, (k - 1.0) * (q + m), 0.0)
            / jnp.where(beyond, 4.0 * q * q - 1.0, 1.0)
        )
        out += [a, -(a * b)]
    return out


def log_scale(order):
    k = (
        lax.broadcasted_iota(jnp.int32, (16, 128), 0) * 128
        + lax.broadcasted_iota(jnp.int32, (16, 128), 1)
        + 1
    )
    terms = jnp.log(1.0 + 0.5 / k.astype(F32))
    return 0.5 * (jnp.sum(jnp.where(k <= order, terms, 0.0)) - math.log(2.0))


def kernel(pair_ref, sines_ref, spec_ref, o_ref, spec, chain, weights, odd, sent, spec_sem, send_sem, recv_sem, own_sem):
    lat, ma = lax.axis_index("lat"), lax.axis_index("ma")
    core, x, y = lax.rem(lat, 2), ma // 2, lax.rem(ma, 2)
    base = lat - core
    sign = jnp.where(lat < 16, 1.0, -1.0).astype(F32)

    def load(s):
        return pltpu.make_async_copy(spec_ref.at[core * SETS + s], spec.at[s], spec_sem.at[s])

    for s in range(SETS):
        load(s).start()

    barrier = pltpu.get_barrier_semaphore()
    for c in range(2):
        for dx in range(4):
            for dy in range(2):
                to = (
                    base + (core if dx + dy == 0 else c),
                    lax.rem(x + dx, 4) * 2 + lax.rem(y + dy, 2),
                )
                if dx + dy > 0:
                    pl.semaphore_signal(barrier, inc=1, device_id=to, device_id_type=MESH)
    pl.semaphore_signal(barrier, inc=1, device_id=(base + 1 - core, ma), device_id_type=MESH)

    seg = lax.broadcasted_iota(jnp.int32, (8, 128), 0)
    lane = lax.broadcasted_iota(jnp.int32, (8, 128), 1)
    starts = seg * SEG
    sines, log_cos = [], []
    for c in range(2):
        at = lax.rem(base, 16) * BAND + c * BAND
        row, skip = at // 128, lax.rem(at, 128)
        here = jnp.broadcast_to(sines_ref[pl.ds(row, 1), :], (8, 128))
        after = jnp.broadcast_to(sines_ref[pl.ds(jnp.minimum(row + 1, 9), 1), :], (8, 128))
        turn = lax.rem(128 - skip, 128)
        value = jnp.where(lane < 128 - skip, pltpu.roll(here, turn, 1), pltpu.roll(after, turn, 1))
        sines.append(value)
        log_cos.append(jnp.log(1.0 - value * value))
        odd[c, pl.ds(NH, 8), :] = jnp.zeros((8, 128), F32)

    row = lax.broadcasted_iota(jnp.int32, (2 * BAND, 128), 0)
    col = lax.broadcasted_iota(jnp.int32, (2 * BAND, 128), 1)
    spread = (row // 2 == col).astype(BF16)

    def one_set(s, _):
        pair = pair_ref[core * SETS + s]
        split = (M + 1 - pair) // 2
        a_even, b_even, a_odd, b_odd = step_factors(pair)
        second = M - 1 - pair
        scale1, scale2 = log_scale(pair), log_scale(second)
        seeds1, seeds2 = [], []
        for c in range(2):
            seeds1.append(jnp.exp(scale1 + 0.5 * pair.astype(F32) * log_cos[c]))
            seeds2.append(jnp.exp(scale2 + 0.5 * second.astype(F32) * log_cos[c]))
        one, zero = jnp.ones((8, 128), F32), jnp.zeros((8, 128), F32)
        state = [[zero, one, one, zero] for c in range(2)]
        for k in range(SEG):
            ae = jnp.broadcast_to(a_even[:, k : k + 1], (8, 128))
            be = jnp.broadcast_to(b_even[:, k : k + 1], (8, 128))
            ao = jnp.broadcast_to(a_odd[:, k : k + 1], (8, 128))
            bo = jnp.broadcast_to(b_odd[:, k : k + 1], (8, 128))
            begins = starts == split - k
            for c in range(2):
                ue, uo, we, wo = state[c]
                axe, axo = ae * sines[c], ao * sines[c]
                ue = axe * uo + (be * ue + jnp.where(begins, seeds2[c], 0.0))
                if k == 0:
                    ue = jnp.where(seg == 0, seeds1[c], ue)
                we = axe * wo + be * we
                uo = axo * ue + bo * uo
                wo = axo * we + bo * wo
                state[c] = [ue, uo, we, wo]
                for i in range(4):
                    chain[c, i, k] = state[c][i]

        ahead = starts - split
        for c in range(2):
            alpha, beta = one, zero
            alphas, betas = one, zero
            for g in range(7):
                ends = [
                    jnp.broadcast_to(chain[c, i, SEG - 1, pl.ds(g, 1), :], (8, 128)) for i in range(4)
                ]
                turned = (g * SEG <= split) & (split < (g + 1) * SEG)
                alpha = jnp.where(turned, 1.0, alpha)
                alpha, beta = alpha * ends[1] + beta * ends[3], alpha * ends[0] + beta * ends[2]
                alphas = jnp.where(seg == g + 1, alpha, alphas)
                betas = jnp.where(seg == g + 1, beta, betas)
            for k in range(SEG):
                scale = jnp.where((ahead <= 0) & (ahead >= -k), 1.0, alphas)
                weights[c, pl.ds(k, 8, stride=SEG), :] = scale * chain[c, 0, k] + betas * chain[c, 2, k]
                odd[c, pl.ds(k, 8, stride=SEG), :] = scale * chain[c, 1, k] + betas * chain[c, 3, k]

        slot = lax.broadcasted_iota(jnp.int32, (NH, 128), 0)
        split_odd = (M - pair) // 2
        moved = slot >= jnp.where(lax.rem(pair, 2) == 1, split_odd, M)
        for c in range(2):
            picked = jnp.where(moved, odd[c, pl.ds(1, NH), :], odd[c, pl.ds(0, NH), :])
            weights[c, pl.ds(NH, NH), :] = sign * picked

        shape = (2 * BAND, 2 * NH)
        which = lax.rem(lax.broadcasted_iota(jnp.int32, shape, 0), 2)
        place = lax.broadcasted_iota(jnp.int32, shape, 1)
        even_part = place < NH
        slots = jnp.where(even_part, place, place - NH)
        cut = jnp.where(even_part, split, split_odd)
        total = jnp.where(even_part, M // 2 + 1, M // 2)
        low = jnp.where(which == 0, 0, cut)
        high = jnp.where(which == 0, cut, total)
        used = (slots >= low) & (slots < high)
        for c in range(2):
            wide = lax.dot_general(
                spread,
                weights[c].astype(BF16),
                (((1,), (1,)), ((), ())),
                preferred_element_type=F32,
            )
            lhs = jnp.where(used, wide, 0.0).astype(BF16)
            if c == 0:
                load(s).wait()
            summed = jnp.dot(lhs, spec[s], preferred_element_type=F32)
            unit = s * 2 + c
            sent[unit] = summed.astype(BF16).reshape(BAND, 2, COLS)
            if c == 0:

                @pl.when(s == 0)
                def _():
                    pl.semaphore_wait(barrier, 15)

            into = o_ref.at[:, ma * 8 + core * SETS + s]
            for dx in (2, 1, 3, 0):
                for dy in (1, 0):
                    to_ma = lax.rem(x + dx, 4) * 2 + lax.rem(y + dy, 2)
                    source = sent.at[unit, pl.ds(to_ma * ROWS, ROWS)]
                    remote = pltpu.make_async_remote_copy(
                        src_ref=source,
                        dst_ref=into,
                        send_sem=send_sem,
                        recv_sem=recv_sem,
                        device_id=(base + c, to_ma),
                        device_id_type=MESH,
                    )
                    if dx + dy > 0:
                        remote.start()
                    else:

                        @pl.when(core == c)
                        def _():
                            pltpu.make_async_copy(source, into, own_sem.at[s]).start()

                        @pl.when(core != c)
                        def _():
                            remote.start()

        return 0

    lax.fori_loop(0, SETS, one_set, 0)

    for s in range(SETS):
        pltpu.make_async_copy(sent.at[0, pl.ds(0, ROWS)], o_ref.at[:, 0], own_sem.at[s]).wait()
    most = o_ref.at[:, pl.ds(0, 60)]
    pltpu.make_async_copy(most, most, send_sem).wait()
    pltpu.make_async_copy(most, most, recv_sem).wait()


def local(spectral, set_pair, lat_sines):
    return pl.pallas_call(
        kernel,
        out_shape=jax.ShapeDtypeStruct((ROWS, 64, 2, COLS), BF16),
        in_specs=[
            pl.BlockSpec(memory_space=pltpu.SMEM),
            pl.BlockSpec(memory_space=pltpu.VMEM),
            pl.BlockSpec(memory_space=pl.ANY),
        ],
        out_specs=pl.BlockSpec(memory_space=pl.ANY),
        scratch_shapes=[
            pltpu.VMEM((SETS, 2 * NH, COLS), BF16),
            pltpu.VMEM((2, 4, SEG, 8, 128), F32),
            pltpu.VMEM((2, 2 * NH, 128), F32),
            pltpu.VMEM((2, NH + 8, 128), F32),
            pltpu.VMEM((2 * SETS, BAND, 2, COLS), BF16),
            pltpu.SemaphoreType.DMA((SETS,)),
            pltpu.SemaphoreType.DMA,
            pltpu.SemaphoreType.DMA,
            pltpu.SemaphoreType.DMA((SETS,)),
        ],
        compiler_params=pltpu.CompilerParams(
            collective_id=0, has_side_effects=True, vmem_limit_bytes=40 * 2**20
        ),
        cost_estimate=pl.CostEstimate(flops=2_600_000_000, bytes_accessed=12_000_000, transcendentals=0),
    )(set_pair, lat_sines.reshape(10, 128), spectral.reshape(8, 2 * NH, COLS))


def solution(mesh):
    placed = (P("ma", None, None, None), P("ma"), P())
    return jax.shard_map(
        local,
        mesh=mesh,
        in_specs=placed,
        out_specs=P(("lat", "ma"), None, None, None),
        check_vma=False,
    )
```

```python
import functools
import math

import jax
import jax.numpy as jnp
from jax import lax
from jax.experimental import pallas as pl
from jax.experimental.pallas import tpu as pltpu
from jax.sharding import PartitionSpec as P

M = 1280
NH = 648
COLS = 768
BAND = 80
ROWS = 10
SEG = 81
SETS = 4
MESH = pl.DeviceIdType.MESH
ORDER = [(dx, dy) for dx in (2, 1, 3, 0) for dy in (1, 0)]
CUTS = 2
F32, BF16 = jnp.float32, jnp.bfloat16


def step_factors(pair):
    seg = lax.broadcasted_iota(jnp.int32, (8, 128), 0)
    lane = lax.broadcasted_iota(jnp.int32, (8, 128), 1)
    v = seg * SEG + lane
    split = (M + 1 - pair) // 2
    first = v < split
    order = jnp.where(first, pair, M - 1 - pair)
    offset = 2 * jnp.where(first, v, v - split)
    out = []
    for parity in range(2):
        k = (offset + parity).astype(F32)
        m = order.astype(F32)
        n = m + k
        num = 4.0 * n * n - 1.0
        den = k * (n + m)
        recurring = k > 0.5
        a = jnp.sqrt(jnp.where(recurring, num, 0.0) / jnp.where(recurring, den, 1.0))
        beyond = k > 1.5
        q = n - 1.0
        b = jnp.sqrt(
            jnp.where(beyond, (k - 1.0) * (q + m), 0.0)
            / jnp.where(beyond, 4.0 * q * q - 1.0, 1.0)
        )
        out += [a, -(a * b)]
    return out


def log_scale(order):
    k = (
        lax.broadcasted_iota(jnp.int32, (16, 128), 0) * 128
        + lax.broadcasted_iota(jnp.int32, (16, 128), 1)
        + 1
    )
    terms = jnp.log(1.0 + 0.5 / k.astype(F32))
    return 0.5 * (jnp.sum(jnp.where(k <= order, terms, 0.0)) - math.log(2.0))


def kernel(
    pairs_ref, lats_ref, spec_ref, o_ref, pair_ref, sines_ref, spec, chain, weights, odd, sent, small_sem, spec_sem, send_sem, recv_sem, own_sem
):
    lat, ma = lax.axis_index("lat"), lax.axis_index("ma")
    core, x, y = lax.rem(lat, 2), ma // 2, lax.rem(ma, 2)
    base = lat - core
    sign = jnp.where(lat < 16, 1.0, -1.0).astype(F32)

    def load(s):
        return pltpu.make_async_copy(spec_ref.at[core * SETS + s], spec.at[s], spec_sem.at[s])

    small = [
        pltpu.make_async_copy(pairs_ref, pair_ref, small_sem.at[0]),
        pltpu.make_async_copy(lats_ref, sines_ref, small_sem.at[1]),
    ]
    for copy in small:
        copy.start()
    load(0).start()

    barrier = pltpu.get_barrier_semaphore()
    for c in range(2):
        for dx in range(4):
            for dy in range(2):
                to = (
                    base + (core if dx + dy == 0 else c),
                    lax.rem(x + dx, 4) * 2 + lax.rem(y + dy, 2),
                )
                if dx + dy > 0:
                    pl.semaphore_signal(barrier, inc=1, device_id=to, device_id_type=MESH)
    pl.semaphore_signal(barrier, inc=1, device_id=(base + 1 - core, ma), device_id_type=MESH)

    for copy in small:
        copy.wait()
    seg = lax.broadcasted_iota(jnp.int32, (8, 128), 0)
    lane = lax.broadcasted_iota(jnp.int32, (8, 128), 1)
    starts = seg * SEG
    sines, log_cos = [], []
    for c in range(2):
        at = lax.rem(base, 16) * BAND + c * BAND
        row, skip = at // 128, lax.rem(at, 128)
        here = jnp.broadcast_to(sines_ref[pl.ds(row, 1), :], (8, 128))
        after = jnp.broadcast_to(sines_ref[pl.ds(jnp.minimum(row + 1, 9), 1), :], (8, 128))
        turn = lax.rem(128 - skip, 128)
        value = jnp.where(lane < 128 - skip, pltpu.roll(here, turn, 1), pltpu.roll(after, turn, 1))
        sines.append(value)
        log_cos.append(jnp.log(1.0 - value * value))
        odd[c, pl.ds(NH, 8), :] = jnp.zeros((8, 128), F32)

    row = lax.broadcasted_iota(jnp.int32, (2 * BAND, 128), 0)
    col = lax.broadcasted_iota(jnp.int32, (2 * BAND, 128), 1)
    place = jnp.zeros((2 * BAND, 128), jnp.int32)
    for d, (dx, dy) in enumerate(ORDER):
        to_ma = lax.rem(x + dx, 4) * 2 + lax.rem(y + dy, 2)
        place = jnp.where(row >= d * 2 * ROWS, to_ma * ROWS - d * ROWS, place)
    spread = (row // 2 + place == col).astype(BF16)

    def one_set(s, _):
        pair = pair_ref[core * SETS + s]
        split = (M + 1 - pair) // 2
        a_even, b_even, a_odd, b_odd = step_factors(pair)
        second = M - 1 - pair
        scale1, scale2 = log_scale(pair), log_scale(second)
        seeds1, seeds2 = [], []
        for c in range(2):
            seeds1.append(jnp.exp(scale1 + 0.5 * pair.astype(F32) * log_cos[c]))
            seeds2.append(jnp.exp(scale2 + 0.5 * second.astype(F32) * log_cos[c]))
        one, zero = jnp.ones((8, 128), F32), jnp.zeros((8, 128), F32)
        state = [[zero, one, one, zero] for c in range(2)]
        for k in range(SEG):
            ae = jnp.broadcast_to(a_even[:, k : k + 1], (8, 128))
            be = jnp.broadcast_to(b_even[:, k : k + 1], (8, 128))
            ao = jnp.broadcast_to(a_odd[:, k : k + 1], (8, 128))
            bo = jnp.broadcast_to(b_odd[:, k : k + 1], (8, 128))
            begins = starts == split - k
            for c in range(2):
                ue, uo, we, wo = state[c]
                axe, axo = ae * sines[c], ao * sines[c]
                ue = axe * uo + (be * ue + jnp.where(begins, seeds2[c], 0.0))
                if k == 0:
                    ue = jnp.where(seg == 0, seeds1[c], ue)
                we = axe * wo + be * we
                uo = axo * ue + bo * uo
                wo = axo * we + bo * wo
                state[c] = [ue, uo, we, wo]
                for i in range(4):
                    chain[c, i, k] = state[c][i]

        ahead = starts - split
        for c in range(2):
            alpha, beta = one, zero
            alphas, betas = one, zero
            for g in range(7):
                ends = [
                    jnp.broadcast_to(chain[c, i, SEG - 1, pl.ds(g, 1), :], (8, 128)) for i in range(4)
                ]
                turned = (g * SEG <= split) & (split < (g + 1) * SEG)
                alpha = jnp.where(turned, 1.0, alpha)
                alpha, beta = alpha * ends[1] + beta * ends[3], alpha * ends[0] + beta * ends[2]
                alphas = jnp.where(seg == g + 1, alpha, alphas)
                betas = jnp.where(seg == g + 1, beta, betas)
            for k in range(SEG):
                scale = jnp.where((ahead <= 0) & (ahead >= -k), 1.0, alphas)
                weights[c, pl.ds(k, 8, stride=SEG), :] = scale * chain[c, 0, k] + betas * chain[c, 2, k]
                odd[c, pl.ds(k, 8, stride=SEG), :] = scale * chain[c, 1, k] + betas * chain[c, 3, k]

        slot = lax.broadcasted_iota(jnp.int32, (NH, 128), 0)
        split_odd = (M - pair) // 2
        moved = slot >= jnp.where(lax.rem(pair, 2) == 1, split_odd, M)
        for c in range(2):
            picked = jnp.where(moved, odd[c, pl.ds(1, NH), :], odd[c, pl.ds(0, NH), :])
            weights[c, pl.ds(NH, NH), :] = sign * picked

        shape = (2 * BAND, 2 * NH)
        which = lax.rem(lax.broadcasted_iota(jnp.int32, shape, 0), 2)
        place = lax.broadcasted_iota(jnp.int32, shape, 1)
        even_part = place < NH
        slots = jnp.where(even_part, place, place - NH)
        cut = jnp.where(even_part, split, split_odd)
        total = jnp.where(even_part, M // 2 + 1, M // 2)
        low = jnp.where(which == 0, 0, cut)
        high = jnp.where(which == 0, cut, total)
        used = (slots >= low) & (slots < high)
        for c in range(2):
            wide = lax.dot_general(
                spread,
                weights[c].astype(BF16),
                (((1,), (1,)), ((), ())),
                preferred_element_type=F32,
            )
            lhs = jnp.where(used, wide, 0.0).astype(BF16)
            if c == 0:
                load(s).wait()

                @pl.when(s + 1 < SETS)
                def _():
                    load(s + 1).start()

            unit = s * 2 + c
            into = o_ref.at[:, ma * 8 + core * SETS + s]
            height = 2 * BAND // CUTS
            for h in range(CUTS):
                summed = jnp.dot(
                    lhs[h * height : (h + 1) * height], spec[s], preferred_element_type=F32
                )
                sent[unit, pl.ds(h * height // 2, height // 2)] = summed.astype(BF16).reshape(
                    height // 2, 2, COLS
                )
                if c == 0 and h == 0:

                    @pl.when(s == 0)
                    def _():
                        pl.semaphore_wait(barrier, 15)

                for d in range(h * 8 // CUTS, (h + 1) * 8 // CUTS):
                    dx, dy = ORDER[d]
                    to_ma = lax.rem(x + dx, 4) * 2 + lax.rem(y + dy, 2)
                    source = sent.at[unit, pl.ds(d * ROWS, ROWS)]
                    remote = pltpu.make_async_remote_copy(
                        src_ref=source,
                        dst_ref=into,
                        send_sem=send_sem,
                        recv_sem=recv_sem,
                        device_id=(base + c, to_ma),
                        device_id_type=MESH,
                    )
                    if dx + dy > 0:
                        remote.start()
                    else:

                        @pl.when(core == c)
                        def _():
                            pltpu.make_async_copy(source, into, own_sem.at[s]).start()

                        @pl.when(core != c)
                        def _():
                            remote.start()

        return 0

    lax.fori_loop(0, SETS, one_set, 0)

    for s in range(SETS):
        pltpu.make_async_copy(sent.at[0, pl.ds(0, ROWS)], o_ref.at[:, 0], own_sem.at[s]).wait()
    most = o_ref.at[:, pl.ds(0, 60)]
    pltpu.make_async_copy(most, most, send_sem).wait()
    pltpu.make_async_copy(most, most, recv_sem).wait()


def in_hbm(array):
    return pltpu.with_memory_space_constraint(array, pltpu.HBM)


def local(spectral, set_pair, lat_sines):
    return pl.pallas_call(
        kernel,
        out_shape=jax.ShapeDtypeStruct((ROWS, 64, 2, COLS), BF16),
        in_specs=[
            pl.BlockSpec(memory_space=pltpu.HBM),
            pl.BlockSpec(memory_space=pltpu.HBM),
            pl.BlockSpec(memory_space=pl.ANY),
        ],
        out_specs=pl.BlockSpec(memory_space=pl.ANY),
        scratch_shapes=[
            pltpu.SMEM((8,), jnp.int32),
            pltpu.VMEM((10, 128), F32),
            pltpu.VMEM((SETS, 2 * NH, COLS), BF16),
            pltpu.VMEM((2, 4, SEG, 8, 128), F32),
            pltpu.VMEM((2, 2 * NH, 128), F32),
            pltpu.VMEM((2, NH + 8, 128), F32),
            pltpu.VMEM((2 * SETS, BAND, 2, COLS), BF16),
            pltpu.SemaphoreType.DMA((2,)),
            pltpu.SemaphoreType.DMA((SETS,)),
            pltpu.SemaphoreType.DMA,
            pltpu.SemaphoreType.DMA,
            pltpu.SemaphoreType.DMA((SETS,)),
        ],
        compiler_params=pltpu.CompilerParams(
            collective_id=0, has_side_effects=True, vmem_limit_bytes=40 * 2**20
        ),
        cost_estimate=pl.CostEstimate(flops=2_600_000_000, bytes_accessed=12_000_000, transcendentals=0),
    )(in_hbm(set_pair), in_hbm(lat_sines.reshape(10, 128)), spectral.reshape(8, 2 * NH, COLS))


def solution(mesh):
    placed = (P("ma", None, None, None), P("ma"), P())
    return jax.shard_map(
        local,
        mesh=mesh,
        in_specs=placed,
        out_specs=P(("lat", "ma"), None, None, None),
        check_vma=False,
    )
```

```python
import functools
import math

import jax
import jax.numpy as jnp
from jax import lax
from jax.experimental import pallas as pl
from jax.experimental.pallas import tpu as pltpu
from jax.sharding import PartitionSpec as P

M = 1280
NH = 648
COLS = 768
BAND = 80
ROWS = 10
SEG = 81
SETS = 8
MESH = pl.DeviceIdType.MESH
ORDER = [(dx, dy) for dx in (2, 1, 3, 0) for dy in (1, 0)]
CUTS = 2
F32, BF16 = jnp.float32, jnp.bfloat16


def step_factors(pair):
    seg = lax.broadcasted_iota(jnp.int32, (8, 128), 0)
    lane = lax.broadcasted_iota(jnp.int32, (8, 128), 1)
    v = seg * SEG + lane
    split = (M + 1 - pair) // 2
    first = v < split
    order = jnp.where(first, pair, M - 1 - pair)
    offset = 2 * jnp.where(first, v, v - split)
    out = []
    for parity in range(2):
        k = (offset + parity).astype(F32)
        m = order.astype(F32)
        n = m + k
        num = 4.0 * n * n - 1.0
        den = k * (n + m)
        recurring = k > 0.5
        a = jnp.sqrt(jnp.where(recurring, num, 0.0) / jnp.where(recurring, den, 1.0))
        beyond = k > 1.5
        q = n - 1.0
        b = jnp.sqrt(
            jnp.where(beyond, (k - 1.0) * (q + m), 0.0)
            / jnp.where(beyond, 4.0 * q * q - 1.0, 1.0)
        )
        out += [a, -(a * b)]
    return out


def log_scale(order):
    k = (
        lax.broadcasted_iota(jnp.int32, (16, 128), 0) * 128
        + lax.broadcasted_iota(jnp.int32, (16, 128), 1)
        + 1
    )
    terms = jnp.log(1.0 + 0.5 / k.astype(F32))
    return 0.5 * (jnp.sum(jnp.where(k <= order, terms, 0.0)) - math.log(2.0))


def kernel(
    pairs_ref, lats_ref, spec_ref, o_ref, pair_ref, sines_ref, spec, chain, weights, odd, sent, small_sem, spec_sem, send_sem, recv_sem, own_sem
):
    lat, ma = lax.axis_index("lat"), lax.axis_index("ma")
    x, y = ma // 2, lax.rem(ma, 2)
    sign = jnp.where(lat < 16, 1.0, -1.0).astype(F32)

    def load(s):
        return pltpu.make_async_copy(spec_ref.at[s], spec.at[s], spec_sem.at[s])

    small = [
        pltpu.make_async_copy(pairs_ref, pair_ref, small_sem.at[0]),
        pltpu.make_async_copy(lats_ref, sines_ref, small_sem.at[1]),
    ]
    for copy in small:
        copy.start()
    load(0).start()

    barrier = pltpu.get_barrier_semaphore()
    for dx, dy in ORDER[:-1]:
        to = (lat, lax.rem(x + dx, 4) * 2 + lax.rem(y + dy, 2))
        pl.semaphore_signal(barrier, inc=1, device_id=to, device_id_type=MESH)

    for copy in small:
        copy.wait()
    seg = lax.broadcasted_iota(jnp.int32, (8, 128), 0)
    lane = lax.broadcasted_iota(jnp.int32, (8, 128), 1)
    starts = seg * SEG
    at = lax.rem(lat, 16) * BAND
    row, skip = at // 128, lax.rem(at, 128)
    here = jnp.broadcast_to(sines_ref[pl.ds(row, 1), :], (8, 128))
    after = jnp.broadcast_to(sines_ref[pl.ds(jnp.minimum(row + 1, 9), 1), :], (8, 128))
    turn = lax.rem(128 - skip, 128)
    sines = jnp.where(lane < 128 - skip, pltpu.roll(here, turn, 1), pltpu.roll(after, turn, 1))
    log_cos = jnp.log(1.0 - sines * sines)
    odd[pl.ds(NH, 8), :] = jnp.zeros((8, 128), F32)

    row = lax.broadcasted_iota(jnp.int32, (2 * BAND, 128), 0)
    col = lax.broadcasted_iota(jnp.int32, (2 * BAND, 128), 1)
    place = jnp.zeros((2 * BAND, 128), jnp.int32)
    for d, (dx, dy) in enumerate(ORDER):
        to_ma = lax.rem(x + dx, 4) * 2 + lax.rem(y + dy, 2)
        place = jnp.where(row >= d * 2 * ROWS, to_ma * ROWS - d * ROWS, place)
    spread = (row // 2 + place == col).astype(BF16)

    def one_set(s, _):
        pair = pair_ref[s]
        split = (M + 1 - pair) // 2
        a_even, b_even, a_odd, b_odd = step_factors(pair)
        second = M - 1 - pair
        seed1 = jnp.exp(log_scale(pair) + 0.5 * pair.astype(F32) * log_cos)
        seed2 = jnp.exp(log_scale(second) + 0.5 * second.astype(F32) * log_cos)
        one, zero = jnp.ones((8, 128), F32), jnp.zeros((8, 128), F32)
        ue, uo, we, wo = zero, one, one, zero
        for k in range(SEG):
            ae = jnp.broadcast_to(a_even[:, k : k + 1], (8, 128)) * sines
            be = jnp.broadcast_to(b_even[:, k : k + 1], (8, 128))
            ao = jnp.broadcast_to(a_odd[:, k : k + 1], (8, 128)) * sines
            bo = jnp.broadcast_to(b_odd[:, k : k + 1], (8, 128))
            ue = ae * uo + (be * ue + jnp.where(starts == split - k, seed2, 0.0))
            if k == 0:
                ue = jnp.where(seg == 0, seed1, ue)
            we = ae * wo + be * we
            uo = ao * ue + bo * uo
            wo = ao * we + bo * wo
            for i, value in enumerate((ue, uo, we, wo)):
                chain[i, k] = value

        ahead = starts - split
        alpha, beta = one, zero
        alphas, betas = one, zero
        for g in range(7):
            ends = [jnp.broadcast_to(chain[i, SEG - 1, pl.ds(g, 1), :], (8, 128)) for i in range(4)]
            turned = (g * SEG <= split) & (split < (g + 1) * SEG)
            alpha = jnp.where(turned, 1.0, alpha)
            alpha, beta = alpha * ends[1] + beta * ends[3], alpha * ends[0] + beta * ends[2]
            alphas = jnp.where(seg == g + 1, alpha, alphas)
            betas = jnp.where(seg == g + 1, beta, betas)
        for k in range(SEG):
            scale = jnp.where((ahead <= 0) & (ahead >= -k), 1.0, alphas)
            weights[pl.ds(k, 8, stride=SEG), :] = scale * chain[0, k] + betas * chain[2, k]
            odd[pl.ds(k, 8, stride=SEG), :] = scale * chain[1, k] + betas * chain[3, k]

        slot = lax.broadcasted_iota(jnp.int32, (NH, 128), 0)
        split_odd = (M - pair) // 2
        moved = slot >= jnp.where(lax.rem(pair, 2) == 1, split_odd, M)
        picked = jnp.where(moved, odd[pl.ds(1, NH), :], odd[pl.ds(0, NH), :])
        weights[pl.ds(NH, NH), :] = sign * picked

        shape = (2 * BAND, 2 * NH)
        which = lax.rem(lax.broadcasted_iota(jnp.int32, shape, 0), 2)
        place = lax.broadcasted_iota(jnp.int32, shape, 1)
        even_part = place < NH
        slots = jnp.where(even_part, place, place - NH)
        cut = jnp.where(even_part, split, split_odd)
        total = jnp.where(even_part, M // 2 + 1, M // 2)
        low = jnp.where(which == 0, 0, cut)
        high = jnp.where(which == 0, cut, total)
        used = (slots >= low) & (slots < high)
        wide = lax.dot_general(
            spread, weights[...].astype(BF16), (((1,), (1,)), ((), ())), preferred_element_type=F32
        )
        lhs = jnp.where(used, wide, 0.0).astype(BF16)
        load(s).wait()

        @pl.when(s + 1 < SETS)
        def _():
            load(s + 1).start()

        into = o_ref.at[:, ma * 8 + s]
        height = 2 * BAND // CUTS
        for h in range(CUTS):
            summed = jnp.dot(lhs[h * height : (h + 1) * height], spec[s], preferred_element_type=F32)
            sent[s, pl.ds(h * height // 2, height // 2)] = summed.astype(BF16).reshape(
                height // 2, 2, COLS
            )
            if h == 0:

                @pl.when(s == 0)
                def _():
                    pl.semaphore_wait(barrier, 7)

            for d in range(h * 8 // CUTS, (h + 1) * 8 // CUTS):
                dx, dy = ORDER[d]
                source = sent.at[s, pl.ds(d * ROWS, ROWS)]
                if dx + dy > 0:
                    pltpu.make_async_remote_copy(
                        src_ref=source,
                        dst_ref=into,
                        send_sem=send_sem,
                        recv_sem=recv_sem,
                        device_id=(lat, lax.rem(x + dx, 4) * 2 + lax.rem(y + dy, 2)),
                        device_id_type=MESH,
                    ).start()
                else:
                    pltpu.make_async_copy(source, into, own_sem.at[s]).start()
        return 0

    lax.fori_loop(0, SETS, one_set, 0)

    for s in range(SETS):
        pltpu.make_async_copy(sent.at[0, pl.ds(0, ROWS)], o_ref.at[:, 0], own_sem.at[s]).wait()
    most = o_ref.at[:, pl.ds(0, 56)]
    pltpu.make_async_copy(most, most, send_sem).wait()
    pltpu.make_async_copy(most, most, recv_sem).wait()


def in_hbm(array):
    return pltpu.with_memory_space_constraint(array, pltpu.HBM)


def local(spectral, set_pair, lat_sines):
    return pl.pallas_call(
        kernel,
        out_shape=jax.ShapeDtypeStruct((ROWS, 64, 2, COLS), BF16),
        in_specs=[
            pl.BlockSpec(memory_space=pltpu.HBM),
            pl.BlockSpec(memory_space=pltpu.HBM),
            pl.BlockSpec(memory_space=pl.ANY),
        ],
        out_specs=pl.BlockSpec(memory_space=pl.ANY),
        scratch_shapes=[
            pltpu.SMEM((8,), jnp.int32),
            pltpu.VMEM((10, 128), F32),
            pltpu.VMEM((SETS, 2 * NH, COLS), BF16),
            pltpu.VMEM((4, SEG, 8, 128), F32),
            pltpu.VMEM((2 * NH, 128), F32),
            pltpu.VMEM((NH + 8, 128), F32),
            pltpu.VMEM((SETS, BAND, 2, COLS), BF16),
            pltpu.SemaphoreType.DMA((2,)),
            pltpu.SemaphoreType.DMA((SETS,)),
            pltpu.SemaphoreType.DMA,
            pltpu.SemaphoreType.DMA,
            pltpu.SemaphoreType.DMA((SETS,)),
        ],
        compiler_params=pltpu.CompilerParams(
            collective_id=0, has_side_effects=True, vmem_limit_bytes=40 * 2**20
        ),
        cost_estimate=pl.CostEstimate(flops=2_600_000_000, bytes_accessed=20_000_000, transcendentals=0),
    )(in_hbm(set_pair), in_hbm(lat_sines.reshape(10, 128)), spectral.reshape(8, 2 * NH, COLS))


def solution(mesh):
    placed = (P("ma", None, None, None), P("ma"), P())
    return jax.shard_map(
        local,
        mesh=mesh,
        in_specs=placed,
        out_specs=P(("lat", "ma"), None, None, None),
        check_vma=False,
    )
```

```python
import functools
import math

import jax
import jax.numpy as jnp
from jax import lax
from jax.experimental import pallas as pl
from jax.experimental.pallas import tpu as pltpu
from jax.sharding import PartitionSpec as P

M = 1280
NH = 648
COLS = 768
BAND = 80
ROWS = 10
SEG = 81
SETS = 8
MESH = pl.DeviceIdType.MESH
ORDER = [(dx, dy) for dx in (2, 1, 3, 0) for dy in (1, 0)]
CUTS = 2
F32, BF16 = jnp.float32, jnp.bfloat16


def step_factors(pair):
    seg = lax.broadcasted_iota(jnp.int32, (8, 128), 0)
    lane = lax.broadcasted_iota(jnp.int32, (8, 128), 1)
    v = seg * SEG + lane
    split = (M + 1 - pair) // 2
    first = v < split
    order = jnp.where(first, pair, M - 1 - pair)
    offset = 2 * jnp.where(first, v, v - split)
    out = []
    for parity in range(2):
        k = (offset + parity).astype(F32)
        m = order.astype(F32)
        n = m + k
        num = 4.0 * n * n - 1.0
        den = k * (n + m)
        recurring = k > 0.5
        a = jnp.sqrt(jnp.where(recurring, num, 0.0) / jnp.where(recurring, den, 1.0))
        beyond = k > 1.5
        q = n - 1.0
        b = jnp.sqrt(
            jnp.where(beyond, (k - 1.0) * (q + m), 0.0)
            / jnp.where(beyond, 4.0 * q * q - 1.0, 1.0)
        )
        out += [a, -(a * b)]
    return out


def log_terms():
    k = (
        lax.broadcasted_iota(jnp.int32, (16, 128), 0) * 128
        + lax.broadcasted_iota(jnp.int32, (16, 128), 1)
        + 1
    )
    return k, jnp.log(1.0 + 0.5 / k.astype(F32))


def log_scale(table, order):
    k, terms = table
    return 0.5 * (jnp.sum(jnp.where(k <= order, terms, 0.0)) - math.log(2.0))


def kernel(
    pairs_ref, lats_ref, spec_ref, o_ref, pair_ref, sines_ref, spec, chain, weights, odd, sent, small_sem, spec_sem, send_sem, recv_sem, own_sem
):
    lat, ma = lax.axis_index("lat"), lax.axis_index("ma")
    x, y = ma // 2, lax.rem(ma, 2)
    sign = jnp.where(lat < 16, 1.0, -1.0).astype(F32)

    def load(s):
        return pltpu.make_async_copy(spec_ref.at[s], spec.at[s], spec_sem.at[s])

    small = [
        pltpu.make_async_copy(pairs_ref, pair_ref, small_sem.at[0]),
        pltpu.make_async_copy(lats_ref, sines_ref, small_sem.at[1]),
    ]
    for copy in small:
        copy.start()
    load(0).start()

    barrier = pltpu.get_barrier_semaphore()
    for dx, dy in ORDER[:-1]:
        to = (lat, lax.rem(x + dx, 4) * 2 + lax.rem(y + dy, 2))
        pl.semaphore_signal(barrier, inc=1, device_id=to, device_id_type=MESH)

    row = lax.broadcasted_iota(jnp.int32, (2 * BAND, 128), 0)
    col = lax.broadcasted_iota(jnp.int32, (2 * BAND, 128), 1)
    place = jnp.zeros((2 * BAND, 128), jnp.int32)
    for d, (dx, dy) in enumerate(ORDER):
        to_ma = lax.rem(x + dx, 4) * 2 + lax.rem(y + dy, 2)
        place = jnp.where(row >= d * 2 * ROWS, to_ma * ROWS - d * ROWS, place)
    spread = (row // 2 + place == col).astype(BF16)
    table = log_terms()
    which = lax.broadcasted_iota(jnp.int32, (8, 2 * NH), 0) & 1
    column = lax.broadcasted_iota(jnp.int32, (8, 2 * NH), 1)

    for copy in small:
        copy.wait()
    seg = lax.broadcasted_iota(jnp.int32, (8, 128), 0)
    lane = lax.broadcasted_iota(jnp.int32, (8, 128), 1)
    starts = seg * SEG
    at = lax.rem(lat, 16) * BAND
    row, skip = at // 128, lax.rem(at, 128)
    here = jnp.broadcast_to(sines_ref[pl.ds(row, 1), :], (8, 128))
    after = jnp.broadcast_to(sines_ref[pl.ds(jnp.minimum(row + 1, 9), 1), :], (8, 128))
    turn = lax.rem(128 - skip, 128)
    sines = jnp.where(lane < 128 - skip, pltpu.roll(here, turn, 1), pltpu.roll(after, turn, 1))
    log_cos = jnp.log(1.0 - sines * sines)
    odd[pl.ds(NH, 8), :] = jnp.zeros((8, 128), F32)

    def one_set(s, _):
        pair = pair_ref[s]
        split = (M + 1 - pair) // 2
        a_even, b_even, a_odd, b_odd = step_factors(pair)
        second = M - 1 - pair
        one, zero = jnp.ones((8, 128), F32), jnp.zeros((8, 128), F32)
        ue, uo, we, wo = zero, one, one, zero
        for k in range(SEG):
            ae = jnp.broadcast_to(a_even[:, k : k + 1], (8, 128)) * sines
            be = jnp.broadcast_to(b_even[:, k : k + 1], (8, 128))
            ao = jnp.broadcast_to(a_odd[:, k : k + 1], (8, 128)) * sines
            bo = jnp.broadcast_to(b_odd[:, k : k + 1], (8, 128))
            ue = ae * uo + (be * ue + jnp.where(starts == split - k, 1.0, 0.0))
            if k == 0:
                ue = jnp.where(seg == 0, 1.0, ue)
            we = ae * wo + be * we
            uo = ao * ue + bo * uo
            wo = ao * we + bo * wo
            for i, value in enumerate((ue, uo, we, wo)):
                chain[i, k] = value

        seed1 = jnp.exp(log_scale(table, pair) + 0.5 * pair.astype(F32) * log_cos)
        seed2 = jnp.exp(log_scale(table, second) + 0.5 * second.astype(F32) * log_cos)
        ahead = starts - split
        alpha, beta = seed1, zero
        alphas, betas = seed1, zero
        for g in range(7):
            ends = [jnp.broadcast_to(chain[i, SEG - 1, pl.ds(g, 1), :], (8, 128)) for i in range(4)]
            turned = (g * SEG <= split) & (split < (g + 1) * SEG)
            alpha = jnp.where(turned, seed2, alpha)
            alpha, beta = alpha * ends[1] + beta * ends[3], alpha * ends[0] + beta * ends[2]
            alphas = jnp.where(seg == g + 1, alpha, alphas)
            betas = jnp.where(seg == g + 1, beta, betas)
        for k in range(SEG):
            scale = jnp.where((ahead <= 0) & (ahead >= -k), seed2, alphas)
            weights[pl.ds(k, 8, stride=SEG), :] = scale * chain[0, k] + betas * chain[2, k]
            odd[pl.ds(k, 8, stride=SEG), :] = scale * chain[1, k] + betas * chain[3, k]

        slot = lax.broadcasted_iota(jnp.int32, (NH, 128), 0)
        split_odd = (M - pair) // 2
        moved = slot >= jnp.where(lax.rem(pair, 2) == 1, split_odd, M)
        picked = jnp.where(moved, odd[pl.ds(1, NH), :], odd[pl.ds(0, NH), :])
        weights[pl.ds(NH, NH), :] = sign * picked

        even_part = column < NH
        slots = jnp.where(even_part, column, column - NH)
        cut = jnp.where(even_part, split, split_odd)
        total = jnp.where(even_part, M // 2 + 1, M // 2)
        low = jnp.where(which == 0, 0, cut)
        high = jnp.where(which == 0, cut, total)
        used = (slots >= low) & (slots < high)
        wide = lax.dot_general(
            spread, weights[...].astype(BF16), (((1,), (1,)), ((), ())), preferred_element_type=F32
        )
        lhs = jnp.where(used[None], wide.reshape(2 * BAND // 8, 8, 2 * NH), 0.0)
        lhs = lhs.reshape(2 * BAND, 2 * NH).astype(BF16)
        load(s).wait()

        @pl.when(s + 1 < SETS)
        def _():
            load(s + 1).start()

        into = o_ref.at[:, ma * 8 + s]
        height = 2 * BAND // CUTS
        for h in range(CUTS):
            summed = jnp.dot(lhs[h * height : (h + 1) * height], spec[s], preferred_element_type=F32)
            sent[s, pl.ds(h * height // 2, height // 2)] = summed.astype(BF16).reshape(
                height // 2, 2, COLS
            )
            if h == 0:

                @pl.when(s == 0)
                def _():
                    pl.semaphore_wait(barrier, 7)

            for d in range(h * 8 // CUTS, (h + 1) * 8 // CUTS):
                dx, dy = ORDER[d]
                source = sent.at[s, pl.ds(d * ROWS, ROWS)]
                if dx + dy > 0:
                    pltpu.make_async_remote_copy(
                        src_ref=source,
                        dst_ref=into,
                        send_sem=send_sem,
                        recv_sem=recv_sem,
                        device_id=(lat, lax.rem(x + dx, 4) * 2 + lax.rem(y + dy, 2)),
                        device_id_type=MESH,
                    ).start()
                else:
                    pltpu.make_async_copy(source, into, own_sem.at[s]).start()
        return 0

    lax.fori_loop(0, SETS, one_set, 0)

    for s in range(SETS):
        pltpu.make_async_copy(sent.at[0, pl.ds(0, ROWS)], o_ref.at[:, 0], own_sem.at[s]).wait()
    most = o_ref.at[:, pl.ds(0, 56)]
    pltpu.make_async_copy(most, most, send_sem).wait()
    pltpu.make_async_copy(most, most, recv_sem).wait()


def in_hbm(array):
    return pltpu.with_memory_space_constraint(array, pltpu.HBM)


def local(spectral, set_pair, lat_sines):
    return pl.pallas_call(
        kernel,
        out_shape=jax.ShapeDtypeStruct((ROWS, 64, 2, COLS), BF16),
        in_specs=[
            pl.BlockSpec(memory_space=pltpu.HBM),
            pl.BlockSpec(memory_space=pltpu.HBM),
            pl.BlockSpec(memory_space=pl.ANY),
        ],
        out_specs=pl.BlockSpec(memory_space=pl.ANY),
        scratch_shapes=[
            pltpu.SMEM((8,), jnp.int32),
            pltpu.VMEM((10, 128), F32),
            pltpu.VMEM((SETS, 2 * NH, COLS), BF16),
            pltpu.VMEM((4, SEG, 8, 128), F32),
            pltpu.VMEM((2 * NH, 128), F32),
            pltpu.VMEM((NH + 8, 128), F32),
            pltpu.VMEM((SETS, BAND, 2, COLS), BF16),
            pltpu.SemaphoreType.DMA((2,)),
            pltpu.SemaphoreType.DMA((SETS,)),
            pltpu.SemaphoreType.DMA,
            pltpu.SemaphoreType.DMA,
            pltpu.SemaphoreType.DMA((SETS,)),
        ],
        compiler_params=pltpu.CompilerParams(
            collective_id=0, has_side_effects=True, vmem_limit_bytes=40 * 2**20
        ),
        cost_estimate=pl.CostEstimate(flops=2_600_000_000, bytes_accessed=20_000_000, transcendentals=0),
    )(in_hbm(set_pair), in_hbm(lat_sines.reshape(10, 128)), spectral.reshape(8, 2 * NH, COLS))


def solution(mesh):
    placed = (P("ma", None, None, None), P("ma"), P())
    return jax.shard_map(
        local,
        mesh=mesh,
        in_specs=placed,
        out_specs=P(("lat", "ma"), None, None, None),
        check_vma=False,
    )
```

```python
import functools
import math

import jax
import jax.numpy as jnp
from jax import lax
from jax.experimental import pallas as pl
from jax.experimental.pallas import tpu as pltpu
from jax.sharding import PartitionSpec as P

M = 1280
NH = 648
COLS = 768
BAND = 80
ROWS = 10
SEG = 81
SETS = 8
MESH = pl.DeviceIdType.MESH
ORDER = [(dx, dy) for dx in (2, 1, 3, 0) for dy in (1, 0)]
CUTS = 4
F32, BF16 = jnp.float32, jnp.bfloat16


def step_factors(pair):
    seg = lax.broadcasted_iota(jnp.int32, (8, 128), 0)
    lane = lax.broadcasted_iota(jnp.int32, (8, 128), 1)
    v = seg * SEG + lane
    split = (M + 1 - pair) // 2
    first = v < split
    order = jnp.where(first, pair, M - 1 - pair)
    offset = 2 * jnp.where(first, v, v - split)
    out = []
    for parity in range(2):
        k = (offset + parity).astype(F32)
        m = order.astype(F32)
        n = m + k
        num = 4.0 * n * n - 1.0
        den = k * (n + m)
        recurring = k > 0.5
        a = jnp.sqrt(jnp.where(recurring, num, 0.0) / jnp.where(recurring, den, 1.0))
        beyond = k > 1.5
        q = n - 1.0
        b = jnp.sqrt(
            jnp.where(beyond, (k - 1.0) * (q + m), 0.0)
            / jnp.where(beyond, 4.0 * q * q - 1.0, 1.0)
        )
        out += [a, -(a * b)]
    return out


def log_terms():
    k = (
        lax.broadcasted_iota(jnp.int32, (16, 128), 0) * 128
        + lax.broadcasted_iota(jnp.int32, (16, 128), 1)
        + 1
    )
    return k, jnp.log(1.0 + 0.5 / k.astype(F32))


def log_scale(table, order):
    k, terms = table
    return 0.5 * (jnp.sum(jnp.where(k <= order, terms, 0.0)) - math.log(2.0))


def kernel(
    pairs_ref, lats_ref, spec_ref, o_ref, pair_ref, sines_ref, spec, chain, weights, odd, sent, small_sem, spec_sem, send_sem, recv_sem, own_sem
):
    lat, ma = lax.axis_index("lat"), lax.axis_index("ma")
    x, y = ma // 2, lax.rem(ma, 2)
    sign = jnp.where(lat < 16, 1.0, -1.0).astype(F32)

    def load(s):
        return pltpu.make_async_copy(spec_ref.at[s], spec.at[s], spec_sem.at[s])

    small = [
        pltpu.make_async_copy(pairs_ref, pair_ref, small_sem.at[0]),
        pltpu.make_async_copy(lats_ref, sines_ref, small_sem.at[1]),
    ]
    for copy in small:
        copy.start()
    load(0).start()

    barrier = pltpu.get_barrier_semaphore()
    for dx, dy in ORDER[:-1]:
        to = (lat, lax.rem(x + dx, 4) * 2 + lax.rem(y + dy, 2))
        pl.semaphore_signal(barrier, inc=1, device_id=to, device_id_type=MESH)

    row = lax.broadcasted_iota(jnp.int32, (2 * BAND, 128), 0)
    col = lax.broadcasted_iota(jnp.int32, (2 * BAND, 128), 1)
    place = jnp.zeros((2 * BAND, 128), jnp.int32)
    for d, (dx, dy) in enumerate(ORDER):
        to_ma = lax.rem(x + dx, 4) * 2 + lax.rem(y + dy, 2)
        place = jnp.where(row >= d * 2 * ROWS, to_ma * ROWS - d * ROWS, place)
    spread = (row // 2 + place == col).astype(BF16)
    table = log_terms()
    which = lax.broadcasted_iota(jnp.int32, (8, 2 * NH), 0) & 1
    column = lax.broadcasted_iota(jnp.int32, (8, 2 * NH), 1)

    for copy in small:
        copy.wait()
    seg = lax.broadcasted_iota(jnp.int32, (8, 128), 0)
    lane = lax.broadcasted_iota(jnp.int32, (8, 128), 1)
    starts = seg * SEG
    at = lax.rem(lat, 16) * BAND
    row, skip = at // 128, lax.rem(at, 128)
    here = jnp.broadcast_to(sines_ref[pl.ds(row, 1), :], (8, 128))
    after = jnp.broadcast_to(sines_ref[pl.ds(jnp.minimum(row + 1, 9), 1), :], (8, 128))
    turn = lax.rem(128 - skip, 128)
    sines = jnp.where(lane < 128 - skip, pltpu.roll(here, turn, 1), pltpu.roll(after, turn, 1))
    log_cos = jnp.log(1.0 - sines * sines)
    odd[pl.ds(NH, 8), :] = jnp.zeros((8, 128), F32)

    def one_set(s, _):
        pair = pair_ref[s]
        split = (M + 1 - pair) // 2
        a_even, b_even, a_odd, b_odd = step_factors(pair)
        second = M - 1 - pair
        one, zero = jnp.ones((8, 128), F32), jnp.zeros((8, 128), F32)
        ue, uo, we, wo = zero, one, one, zero
        for k in range(SEG):
            ae = jnp.broadcast_to(a_even[:, k : k + 1], (8, 128)) * sines
            be = jnp.broadcast_to(b_even[:, k : k + 1], (8, 128))
            ao = jnp.broadcast_to(a_odd[:, k : k + 1], (8, 128)) * sines
            bo = jnp.broadcast_to(b_odd[:, k : k + 1], (8, 128))
            ue = ae * uo + (be * ue + jnp.where(starts == split - k, 1.0, 0.0))
            if k == 0:
                ue = jnp.where(seg == 0, 1.0, ue)
            we = ae * wo + be * we
            uo = ao * ue + bo * uo
            wo = ao * we + bo * wo
            for i, value in enumerate((ue, uo, we, wo)):
                chain[i, k] = value

        seed1 = jnp.exp(log_scale(table, pair) + 0.5 * pair.astype(F32) * log_cos)
        seed2 = jnp.exp(log_scale(table, second) + 0.5 * second.astype(F32) * log_cos)
        ahead = starts - split
        alpha, beta = seed1, zero
        alphas, betas = seed1, zero
        for g in range(7):
            ends = [jnp.broadcast_to(chain[i, SEG - 1, pl.ds(g, 1), :], (8, 128)) for i in range(4)]
            turned = (g * SEG <= split) & (split < (g + 1) * SEG)
            alpha = jnp.where(turned, seed2, alpha)
            alpha, beta = alpha * ends[1] + beta * ends[3], alpha * ends[0] + beta * ends[2]
            alphas = jnp.where(seg == g + 1, alpha, alphas)
            betas = jnp.where(seg == g + 1, beta, betas)
        for k in range(SEG):
            scale = jnp.where((ahead <= 0) & (ahead >= -k), seed2, alphas)
            weights[pl.ds(k, 8, stride=SEG), :] = scale * chain[0, k] + betas * chain[2, k]
            odd[pl.ds(k, 8, stride=SEG), :] = scale * chain[1, k] + betas * chain[3, k]

        slot = lax.broadcasted_iota(jnp.int32, (NH, 128), 0)
        split_odd = (M - pair) // 2
        moved = slot >= jnp.where(lax.rem(pair, 2) == 1, split_odd, M)
        picked = jnp.where(moved, odd[pl.ds(1, NH), :], odd[pl.ds(0, NH), :])
        weights[pl.ds(NH, NH), :] = sign * picked

        even_part = column < NH
        slots = jnp.where(even_part, column, column - NH)
        cut = jnp.where(even_part, split, split_odd)
        total = jnp.where(even_part, M // 2 + 1, M // 2)
        low = jnp.where(which == 0, 0, cut)
        high = jnp.where(which == 0, cut, total)
        used = (slots >= low) & (slots < high)
        wide = lax.dot_general(
            spread, weights[...].astype(BF16), (((1,), (1,)), ((), ())), preferred_element_type=F32
        )
        lhs = jnp.where(used[None], wide.reshape(2 * BAND // 8, 8, 2 * NH), 0.0)
        lhs = lhs.reshape(2 * BAND, 2 * NH).astype(BF16)
        load(s).wait()

        @pl.when(s + 1 < SETS)
        def _():
            load(s + 1).start()

        into = o_ref.at[:, ma * 8 + s]
        height = 2 * BAND // CUTS
        for h in range(CUTS):
            summed = jnp.dot(lhs[h * height : (h + 1) * height], spec[s], preferred_element_type=F32)
            sent[s, pl.ds(h * height // 2, height // 2)] = summed.astype(BF16).reshape(
                height // 2, 2, COLS
            )
            if h == 0:

                @pl.when(s == 0)
                def _():
                    pl.semaphore_wait(barrier, 7)

            for d in range(h * 8 // CUTS, (h + 1) * 8 // CUTS):
                dx, dy = ORDER[d]
                source = sent.at[s, pl.ds(d * ROWS, ROWS)]
                if dx + dy > 0:
                    pltpu.make_async_remote_copy(
                        src_ref=source,
                        dst_ref=into,
                        send_sem=send_sem,
                        recv_sem=recv_sem,
                        device_id=(lat, lax.rem(x + dx, 4) * 2 + lax.rem(y + dy, 2)),
                        device_id_type=MESH,
                    ).start()
                else:
                    pltpu.make_async_copy(source, into, own_sem.at[s]).start()
        return 0

    lax.fori_loop(0, SETS, one_set, 0)

    for s in range(SETS):
        pltpu.make_async_copy(sent.at[0, pl.ds(0, ROWS)], o_ref.at[:, 0], own_sem.at[s]).wait()
    most = o_ref.at[:, pl.ds(0, 56)]
    pltpu.make_async_copy(most, most, send_sem).wait()
    pltpu.make_async_copy(most, most, recv_sem).wait()


def in_hbm(array):
    return pltpu.with_memory_space_constraint(array, pltpu.HBM)


def local(spectral, set_pair, lat_sines):
    return pl.pallas_call(
        kernel,
        out_shape=jax.ShapeDtypeStruct((ROWS, 64, 2, COLS), BF16),
        in_specs=[
            pl.BlockSpec(memory_space=pltpu.HBM),
            pl.BlockSpec(memory_space=pltpu.HBM),
            pl.BlockSpec(memory_space=pl.ANY),
        ],
        out_specs=pl.BlockSpec(memory_space=pl.ANY),
        scratch_shapes=[
            pltpu.SMEM((8,), jnp.int32),
            pltpu.VMEM((10, 128), F32),
            pltpu.VMEM((SETS, 2 * NH, COLS), BF16),
            pltpu.VMEM((4, SEG, 8, 128), F32),
            pltpu.VMEM((2 * NH, 128), F32),
            pltpu.VMEM((NH + 8, 128), F32),
            pltpu.VMEM((SETS, BAND, 2, COLS), BF16),
            pltpu.SemaphoreType.DMA((2,)),
            pltpu.SemaphoreType.DMA((SETS,)),
            pltpu.SemaphoreType.DMA,
            pltpu.SemaphoreType.DMA,
            pltpu.SemaphoreType.DMA((SETS,)),
        ],
        compiler_params=pltpu.CompilerParams(
            collective_id=0, has_side_effects=True, vmem_limit_bytes=40 * 2**20
        ),
        cost_estimate=pl.CostEstimate(flops=2_600_000_000, bytes_accessed=20_000_000, transcendentals=0),
    )(in_hbm(set_pair), in_hbm(lat_sines.reshape(10, 128)), spectral.reshape(8, 2 * NH, COLS))


def solution(mesh):
    placed = (P("ma", None, None, None), P("ma"), P())
    return jax.shard_map(
        local,
        mesh=mesh,
        in_specs=placed,
        out_specs=P(("lat", "ma"), None, None, None),
        check_vma=False,
    )
```

```python
import functools
import math

import jax
import jax.numpy as jnp
from jax import lax
from jax.experimental import pallas as pl
from jax.experimental.pallas import tpu as pltpu
from jax.sharding import PartitionSpec as P

M = 1280
NH = 648
COLS = 768
BAND = 80
ROWS = 10
SEG = 81
SETS = 8
MESH = pl.DeviceIdType.MESH
ORDER = [(dx, dy) for dx in (1, 3, 2, 0) for dy in (1, 0)]
CUTS = 2
F32, BF16 = jnp.float32, jnp.bfloat16


def step_factors(pair):
    seg = lax.broadcasted_iota(jnp.int32, (8, 128), 0)
    lane = lax.broadcasted_iota(jnp.int32, (8, 128), 1)
    v = seg * SEG + lane
    split = (M + 1 - pair) // 2
    first = v < split
    order = jnp.where(first, pair, M - 1 - pair)
    offset = 2 * jnp.where(first, v, v - split)
    out = []
    for parity in range(2):
        k = (offset + parity).astype(F32)
        m = order.astype(F32)
        n = m + k
        num = 4.0 * n * n - 1.0
        den = k * (n + m)
        recurring = k > 0.5
        a = jnp.sqrt(jnp.where(recurring, num, 0.0) / jnp.where(recurring, den, 1.0))
        beyond = k > 1.5
        q = n - 1.0
        b = jnp.sqrt(
            jnp.where(beyond, (k - 1.0) * (q + m), 0.0)
            / jnp.where(beyond, 4.0 * q * q - 1.0, 1.0)
        )
        out += [a, -(a * b)]
    return out


def log_terms():
    k = (
        lax.broadcasted_iota(jnp.int32, (16, 128), 0) * 128
        + lax.broadcasted_iota(jnp.int32, (16, 128), 1)
        + 1
    )
    return k, jnp.log(1.0 + 0.5 / k.astype(F32))


def log_scale(table, order):
    k, terms = table
    return 0.5 * (jnp.sum(jnp.where(k <= order, terms, 0.0)) - math.log(2.0))


def kernel(
    pairs_ref, lats_ref, spec_ref, o_ref, pair_ref, sines_ref, spec, chain, weights, odd, sent, small_sem, spec_sem, send_sem, recv_sem, own_sem
):
    lat, ma = lax.axis_index("lat"), lax.axis_index("ma")
    x, y = ma // 2, lax.rem(ma, 2)
    sign = jnp.where(lat < 16, 1.0, -1.0).astype(F32)

    def load(s):
        return pltpu.make_async_copy(spec_ref.at[s], spec.at[s], spec_sem.at[s])

    small = [
        pltpu.make_async_copy(pairs_ref, pair_ref, small_sem.at[0]),
        pltpu.make_async_copy(lats_ref, sines_ref, small_sem.at[1]),
    ]
    for copy in small:
        copy.start()
    load(0).start()

    barrier = pltpu.get_barrier_semaphore()
    for dx, dy in ORDER[:-1]:
        to = (lat, lax.rem(x + dx, 4) * 2 + lax.rem(y + dy, 2))
        pl.semaphore_signal(barrier, inc=1, device_id=to, device_id_type=MESH)

    row = lax.broadcasted_iota(jnp.int32, (2 * BAND, 128), 0)
    col = lax.broadcasted_iota(jnp.int32, (2 * BAND, 128), 1)
    place = jnp.zeros((2 * BAND, 128), jnp.int32)
    for d, (dx, dy) in enumerate(ORDER):
        to_ma = lax.rem(x + dx, 4) * 2 + lax.rem(y + dy, 2)
        place = jnp.where(row >= d * 2 * ROWS, to_ma * ROWS - d * ROWS, place)
    spread = (row // 2 + place == col).astype(BF16)
    table = log_terms()
    which = lax.broadcasted_iota(jnp.int32, (8, 2 * NH), 0) & 1
    column = lax.broadcasted_iota(jnp.int32, (8, 2 * NH), 1)

    for copy in small:
        copy.wait()
    seg = lax.broadcasted_iota(jnp.int32, (8, 128), 0)
    lane = lax.broadcasted_iota(jnp.int32, (8, 128), 1)
    starts = seg * SEG
    at = lax.rem(lat, 16) * BAND
    row, skip = at // 128, lax.rem(at, 128)
    here = jnp.broadcast_to(sines_ref[pl.ds(row, 1), :], (8, 128))
    after = jnp.broadcast_to(sines_ref[pl.ds(jnp.minimum(row + 1, 9), 1), :], (8, 128))
    turn = lax.rem(128 - skip, 128)
    sines = jnp.where(lane < 128 - skip, pltpu.roll(here, turn, 1), pltpu.roll(after, turn, 1))
    log_cos = jnp.log(1.0 - sines * sines)
    odd[pl.ds(NH, 8), :] = jnp.zeros((8, 128), F32)

    def one_set(s, _):
        pair = pair_ref[s]
        split = (M + 1 - pair) // 2
        a_even, b_even, a_odd, b_odd = step_factors(pair)
        second = M - 1 - pair
        one, zero = jnp.ones((8, 128), F32), jnp.zeros((8, 128), F32)
        ue, uo, we, wo = zero, one, one, zero
        for k in range(SEG):
            ae = jnp.broadcast_to(a_even[:, k : k + 1], (8, 128)) * sines
            be = jnp.broadcast_to(b_even[:, k : k + 1], (8, 128))
            ao = jnp.broadcast_to(a_odd[:, k : k + 1], (8, 128)) * sines
            bo = jnp.broadcast_to(b_odd[:, k : k + 1], (8, 128))
            ue = ae * uo + (be * ue + jnp.where(starts == split - k, 1.0, 0.0))
            if k == 0:
                ue = jnp.where(seg == 0, 1.0, ue)
            we = ae * wo + be * we
            uo = ao * ue + bo * uo
            wo = ao * we + bo * wo
            for i, value in enumerate((ue, uo, we, wo)):
                chain[i, k] = value

        seed1 = jnp.exp(log_scale(table, pair) + 0.5 * pair.astype(F32) * log_cos)
        seed2 = jnp.exp(log_scale(table, second) + 0.5 * second.astype(F32) * log_cos)
        ahead = starts - split
        alpha, beta = seed1, zero
        alphas, betas = seed1, zero
        for g in range(7):
            ends = [jnp.broadcast_to(chain[i, SEG - 1, pl.ds(g, 1), :], (8, 128)) for i in range(4)]
            turned = (g * SEG <= split) & (split < (g + 1) * SEG)
            alpha = jnp.where(turned, seed2, alpha)
            alpha, beta = alpha * ends[1] + beta * ends[3], alpha * ends[0] + beta * ends[2]
            alphas = jnp.where(seg == g + 1, alpha, alphas)
            betas = jnp.where(seg == g + 1, beta, betas)
        for k in range(SEG):
            scale = jnp.where((ahead <= 0) & (ahead >= -k), seed2, alphas)
            weights[pl.ds(k, 8, stride=SEG), :] = scale * chain[0, k] + betas * chain[2, k]
            odd[pl.ds(k, 8, stride=SEG), :] = scale * chain[1, k] + betas * chain[3, k]

        slot = lax.broadcasted_iota(jnp.int32, (NH, 128), 0)
        split_odd = (M - pair) // 2
        moved = slot >= jnp.where(lax.rem(pair, 2) == 1, split_odd, M)
        picked = jnp.where(moved, odd[pl.ds(1, NH), :], odd[pl.ds(0, NH), :])
        weights[pl.ds(NH, NH), :] = sign * picked

        even_part = column < NH
        slots = jnp.where(even_part, column, column - NH)
        cut = jnp.where(even_part, split, split_odd)
        total = jnp.where(even_part, M // 2 + 1, M // 2)
        low = jnp.where(which == 0, 0, cut)
        high = jnp.where(which == 0, cut, total)
        used = (slots >= low) & (slots < high)
        wide = lax.dot_general(
            spread, weights[...].astype(BF16), (((1,), (1,)), ((), ())), preferred_element_type=F32
        )
        lhs = jnp.where(used[None], wide.reshape(2 * BAND // 8, 8, 2 * NH), 0.0)
        lhs = lhs.reshape(2 * BAND, 2 * NH).astype(BF16)
        load(s).wait()

        @pl.when(s + 1 < SETS)
        def _():
            load(s + 1).start()

        into = o_ref.at[:, ma * 8 + s]
        height = 2 * BAND // CUTS
        for h in range(CUTS):
            summed = jnp.dot(lhs[h * height : (h + 1) * height], spec[s], preferred_element_type=F32)
            sent[s, pl.ds(h * height // 2, height // 2)] = summed.astype(BF16).reshape(
                height // 2, 2, COLS
            )
            if h == 0:

                @pl.when(s == 0)
                def _():
                    pl.semaphore_wait(barrier, 7)

            for d in range(h * 8 // CUTS, (h + 1) * 8 // CUTS):
                dx, dy = ORDER[d]
                source = sent.at[s, pl.ds(d * ROWS, ROWS)]
                if dx + dy > 0:
                    pltpu.make_async_remote_copy(
                        src_ref=source,
                        dst_ref=into,
                        send_sem=send_sem,
                        recv_sem=recv_sem,
                        device_id=(lat, lax.rem(x + dx, 4) * 2 + lax.rem(y + dy, 2)),
                        device_id_type=MESH,
                    ).start()
                else:
                    pltpu.make_async_copy(source, into, own_sem.at[s]).start()
        return 0

    lax.fori_loop(0, SETS, one_set, 0)

    for s in range(SETS):
        pltpu.make_async_copy(sent.at[0, pl.ds(0, ROWS)], o_ref.at[:, 0], own_sem.at[s]).wait()
    most = o_ref.at[:, pl.ds(0, 56)]
    pltpu.make_async_copy(most, most, send_sem).wait()
    pltpu.make_async_copy(most, most, recv_sem).wait()


def in_hbm(array):
    return pltpu.with_memory_space_constraint(array, pltpu.HBM)


def local(spectral, set_pair, lat_sines):
    return pl.pallas_call(
        kernel,
        out_shape=jax.ShapeDtypeStruct((ROWS, 64, 2, COLS), BF16),
        in_specs=[
            pl.BlockSpec(memory_space=pltpu.HBM),
            pl.BlockSpec(memory_space=pltpu.HBM),
            pl.BlockSpec(memory_space=pl.ANY),
        ],
        out_specs=pl.BlockSpec(memory_space=pl.ANY),
        scratch_shapes=[
            pltpu.SMEM((8,), jnp.int32),
            pltpu.VMEM((10, 128), F32),
            pltpu.VMEM((SETS, 2 * NH, COLS), BF16),
            pltpu.VMEM((4, SEG, 8, 128), F32),
            pltpu.VMEM((2 * NH, 128), F32),
            pltpu.VMEM((NH + 8, 128), F32),
            pltpu.VMEM((SETS, BAND, 2, COLS), BF16),
            pltpu.SemaphoreType.DMA((2,)),
            pltpu.SemaphoreType.DMA((SETS,)),
            pltpu.SemaphoreType.DMA,
            pltpu.SemaphoreType.DMA,
            pltpu.SemaphoreType.DMA((SETS,)),
        ],
        compiler_params=pltpu.CompilerParams(
            collective_id=0, has_side_effects=True, vmem_limit_bytes=40 * 2**20
        ),
        cost_estimate=pl.CostEstimate(flops=2_600_000_000, bytes_accessed=20_000_000, transcendentals=0),
    )(in_hbm(set_pair), in_hbm(lat_sines.reshape(10, 128)), spectral.reshape(8, 2 * NH, COLS))


def solution(mesh):
    placed = (P("ma", None, None, None), P("ma"), P())
    return jax.shard_map(
        local,
        mesh=mesh,
        in_specs=placed,
        out_specs=P(("lat", "ma"), None, None, None),
        check_vma=False,
    )
```
